32 devices in a mesh: dp: 4 (over y, x), tensor: 8 (over z, core).
Axes of the slice: x: 2, y: 2, z: 4, core: 2. Of those that a mesh axis runs over, the one named last changes fastest.
Arguments:
- prefill_state: float32 [16, 256, 64, 128], P('dp', 'tensor'), may hold values from -1.2 to 1.2
- assign: int32 [16], replicated, may hold values from 0 to 15, as said below
- tokens: int32 [16, 2], replicated, may hold values from 0 to 65535
- embed_table: bfloat16 [65536, 8192], P('tensor', 'dp'), may hold values from -6 to 6
- w_xz: bfloat16 [8192, 256, 128], P('dp', 'tensor'), may hold values from -0.0625 to 0.0625
- w_dt: bfloat16 [8192, 256], P('dp', 'tensor'), may hold values from -0.0625 to 0.0625
- w_bc: bfloat16 [8192, 2048], P('dp', 'tensor'), may hold values from -0.0625 to 0.0625
- dt_bias: float32 [256], P('tensor'), may hold values from -3 to 0
- a_log: float32 [256], P('tensor'), may hold values from 0 to 1.5
- d_skip: float32 [256], P('tensor'), may hold values from 0.5 to 2
- norm_w: float32 [256, 64], P('tensor'), may hold values from 0.1 to 1.9
- w_out: bfloat16 [16384, 8192], P('tensor', 'dp'), may hold values from -0.046875 to 0.046875
Outputs:
- layer_out: bfloat16 [16, 2, 8192], P('tensor', None, 'dp')
- decode_state: float32 [4, 8, 64, 2, 64, 128], P('dp', 'tensor')
The draws below stay inside these ranges and needn't reach their ends.
Inputs may be any that keep to these rules, and one draw needn't show every extreme that they name: assign is a permutation; the 4 requests i with i // 4 = s send exactly 1 to the positions p with p // 4 = d, for every s and d.
All inputs are finite; a program needn't handle non-finite values.
Results may differ from the reference program's by a relative error of at most 0.0041.
Values may be sent and summed in bfloat16 or wider, within the bound.
A program may use at most 256 MiB of HBM per device.

```python
import jax
import jax.numpy as jnp
from jax import lax

D = 8192
HEADS = 256
P_SIZE = 64
N = 128
GROUPS = 8
VOCAB = 65536
RANKS = 4
STEPS = 2
GRP_REQ = 2
REQ_DP = 4
PAIR = 1
REQUESTS = 16
N_DP = 4
N_TENSOR = 8


def draw_assign(key, part):
    key = jax.random.fold_in(key, 7)
    owner_key, slot_key = jax.random.split(key)
    owner_base = jnp.arange(REQ_DP, dtype=jnp.int32) // PAIR
    owners = jax.vmap(lambda subkey: jax.random.permutation(subkey, owner_base))(jax.random.split(owner_key, N_DP))
    flattened = owners.reshape(-1)
    positions = jnp.arange(REQUESTS, dtype=jnp.int32)
    grouped = jnp.argsort(flattened * REQUESTS + positions, stable=True).astype(jnp.int32).reshape(N_DP, REQ_DP)
    shuffled = jax.vmap(lambda subkey, values: jax.random.permutation(subkey, values))(jax.random.split(slot_key, N_DP), grouped)
    return shuffled.reshape(-1).astype(jnp.int32)


def place_ends(array, rng, smallest, top_value):
    extent = array.shape
    index_at = [jax.random.randint(jax.random.fold_in(rng, axis), (), 0, extent[axis]) for axis in range(len(extent))]
    array = array.at[tuple(index_at)].set(smallest)
    longest = extent.index(max(extent))
    index_at[longest] = (index_at[longest] + 1) % extent[longest]
    return array.at[tuple(index_at)].set(top_value)


def block_scale(key, dims, cuts, low, high):
    level = 1.0
    for dim, parts in cuts:
        draws = jax.random.uniform(jax.random.fold_in(jax.random.fold_in(key, 6), dim), (parts,), jnp.float32, low / len(cuts), high / len(cuts))
        level = level * jnp.repeat(jnp.exp(draws), dims[dim] // parts).reshape((-1,) + (1,) * (len(dims) - 1 - dim))
    return level


def gaussian(own_key, shape, scale, bound, pieces=(), kind=jnp.bfloat16):
    entries = jax.random.normal(own_key, shape, jnp.float32) * scale
    if len(pieces) > 0:
        entries = block_scale(own_key, shape, pieces, -0.22, 0.18) * entries
    return jnp.clip(entries, min=-bound, max=bound).astype(kind)


def setup_inputs(seed: int = 0) -> dict:
    splits = jax.random.split(jax.random.key(seed), 13)
    return {
        "prefill_state": gaussian(splits[0], (REQUESTS, HEADS, P_SIZE, N), 0.2, 1.2, ((0, 4), (1, 8)), jnp.float32),
        "assign": draw_assign(jax.random.fold_in(splits[12], 71), 0),
        "tokens": place_ends(jax.random.randint(splits[2], (REQUESTS, STEPS), 0, VOCAB), jax.random.fold_in(splits[2], 1), 0, VOCAB - 1).astype(jnp.int32),
        "embed_table": gaussian(splits[3], (VOCAB, D), 1.0, 6.0, ((0, 8), (1, 4))),
        "w_xz": gaussian(splits[4], (D, HEADS, 2 * P_SIZE), D ** -0.5, 0.0625, ((0, 4), (1, 8))),
        "w_dt": gaussian(splits[5], (D, HEADS), D ** -0.5, 0.0625, ((0, 4), (1, 8))),
        "w_bc": gaussian(splits[6], (D, GROUPS * 2 * N), D ** -0.5, 0.0625, ((0, 4), (1, 8))),
        "dt_bias": jnp.clip(-3.0 + 3.0 * jax.random.uniform(splits[7], (HEADS,), jnp.float32) ** block_scale(splits[7], (HEADS,), ((0, 8),), -0.2, 0.2), -3.0, 0.0),
        "a_log": jnp.clip(1.5 * jax.random.uniform(splits[8], (HEADS,), jnp.float32) ** block_scale(splits[8], (HEADS,), ((0, 8),), -0.2, 0.2), 0.0, 1.5),
        "d_skip": jnp.clip(0.5 + 1.5 * jax.random.uniform(splits[9], (HEADS,), jnp.float32) ** block_scale(splits[9], (HEADS,), ((0, 8),), -0.2, 0.2), 0.5, 2.0),
        "norm_w": jnp.clip(1.0 + 0.18 * jax.random.normal(splits[10], (HEADS, P_SIZE), jnp.float32), 0.1, 1.9),
        "w_out": gaussian(splits[11], (HEADS * P_SIZE, D), (HEADS * P_SIZE) ** -0.5, 0.046875, ((0, 8), (1, 4))),
    }


norm_eps = 1e-05

def reference(prefill_state, assign, tokens, embed_table, w_xz, w_dt, w_bc, dt_bias, a_log, d_skip, norm_w, w_out):
    inverse = jnp.argsort(assign).astype(jnp.int32)
    ssm_state = jnp.take(prefill_state, inverse, axis=0)
    tok_pos = jnp.take(tokens, inverse, axis=0)
    emb = jnp.take(embed_table, tok_pos, axis=0)
    flat_emb = emb.reshape(REQUESTS * STEPS, D)
    xz_all = jnp.dot(flat_emb, w_xz.reshape(D, HEADS * 2 * P_SIZE), preferred_element_type=jnp.float32).reshape(REQUESTS, STEPS, HEADS, 2 * P_SIZE)
    raw_dt = jnp.dot(flat_emb, w_dt, preferred_element_type=jnp.float32).reshape(REQUESTS, STEPS, HEADS)
    bc_all = jnp.dot(flat_emb, w_bc, preferred_element_type=jnp.float32).reshape(REQUESTS, STEPS, GROUPS, 2 * N)
    per_group = HEADS // GROUPS
    head_group = (jnp.arange(HEADS) // per_group).astype(jnp.int32)
    bc_heads = jnp.take(bc_all, head_group, axis=2)
    decay_rate = jnp.exp(a_log)
    results = []
    for step_idx in range(STEPS):
        xin = xz_all[:, step_idx, :, :P_SIZE]
        zin = xz_all[:, step_idx, :, P_SIZE:]
        bvec = bc_heads[:, step_idx, :, :N]
        cvec = bc_heads[:, step_idx, :, N:]
        delta = jax.nn.softplus(raw_dt[:, step_idx] + dt_bias)
        decay = jnp.exp(-delta * decay_rate)
        ssm_state = ssm_state * decay[:, :, None, None] + (delta[:, :, None] * xin)[:, :, :, None] * bvec[:, :, None, :]
        yout = lax.optimization_barrier(jnp.sum(ssm_state * cvec[:, :, None, :], axis=-1)) + d_skip[:, None] * xin
        results.append(yout * jax.nn.silu(zin))
    gated = jnp.stack(results, axis=1)
    grouped = gated.reshape(REQUESTS, STEPS, GROUPS, per_group * P_SIZE)
    mean_sq = lax.optimization_barrier(jnp.mean(grouped * grouped, axis=-1, keepdims=True))
    normed = (grouped * lax.rsqrt(mean_sq + norm_eps)).reshape(REQUESTS, STEPS, HEADS, P_SIZE) * norm_w
    normed = normed.astype(jnp.bfloat16)
    mixed = jnp.dot(normed.reshape(REQUESTS * STEPS, HEADS * P_SIZE), w_out, preferred_element_type=jnp.float32).reshape(REQUESTS, STEPS, D)
    layer_out = (emb.astype(jnp.float32) + mixed).astype(jnp.bfloat16)
    head_block = HEADS // N_TENSOR
    rank_heads = head_block // RANKS
    quads = N_TENSOR // RANKS
    shaped = ssm_state.reshape(N_DP, quads, GRP_REQ, N_TENSOR, RANKS, rank_heads, P_SIZE, N)
    moved = jnp.transpose(shaped, (0, 1, 4, 3, 5, 2, 6, 7))
    decode_state = moved.reshape(N_DP, N_TENSOR, HEADS // RANKS, GRP_REQ, P_SIZE, N)
    return (layer_out, decode_state)
```

```python
import jax
import jax.numpy as jnp
from jax import lax
from jax.experimental import pallas as pl
from jax.experimental.pallas import tpu as pltpu
from jax.sharding import PartitionSpec as P

HEADS = 256
GROUPS = 8
RANKS = 4


norm_eps = 1e-05


def partner(value, axis, apart):
    mask = 2**apart
    pairs = [(source, source ^ mask) for source in range(lax.axis_size(axis))]
    return lax.ppermute(value, axis, pairs)


def arrange(value, quads, ranks):
    rest = value.shape[2:]
    group_req = value.shape[0] // quads
    rank_heads = value.shape[1] // ranks
    shaped = value.reshape((quads, group_req, ranks, rank_heads) + rest)
    extra = tuple(range(4, 4 + len(rest)))
    moved = jnp.transpose(shaped, (0, 2, 3, 1) + extra)
    return moved.reshape((quads * ranks, rank_heads, group_req) + rest)


def restore(value, quads, ranks):
    rank_heads = value.shape[1]
    group_req = value.shape[2]
    rest = value.shape[3:]
    shaped = value.reshape((quads, ranks, rank_heads, group_req) + rest)
    extra = tuple(range(4, 4 + len(rest)))
    moved = jnp.transpose(shaped, (0, 3, 1, 2) + extra)
    return moved.reshape((quads * group_req, ranks * rank_heads) + rest)


def advance(ssm_state, inputs, raw_dt, bc_rows, bias, decay_rate, skip):
    steps = raw_dt.shape[-1]
    head_dim = inputs.shape[-1] // 2
    state_dim = bc_rows.shape[-1] // 2
    results = []
    for step_idx in range(steps):
        xin = inputs[..., step_idx, :head_dim]
        zin = inputs[..., step_idx, head_dim:]
        bvec = bc_rows[..., step_idx, :state_dim]
        cvec = bc_rows[..., step_idx, state_dim:]
        delta = jax.nn.softplus(raw_dt[..., step_idx] + bias)
        decay = jnp.exp(-delta * decay_rate)
        ssm_state = (
            ssm_state * decay[..., None, None]
            + (delta[..., None] * xin)[..., :, None] * bvec[..., None, :]
        )
        yout = jnp.sum(ssm_state * cvec[..., None, :], axis=-1) + skip[..., None] * xin
        results.append(yout * jax.nn.silu(zin))
    return (ssm_state, jnp.stack(results, axis=-2))


def group_totals(partial_value, bit_count):
    for bit in range(bit_count):
        partial_value = partial_value + partner(partial_value, "tensor", bit)
    return partial_value


def to_groups(state, assign, dindex, ndp):
    req_dp = state.shape[0]
    pair = req_dp // ndp
    own_pos = lax.dynamic_slice_in_dim(assign, dindex * req_dp, req_dp)
    send_order = jnp.argsort(own_pos)
    outgoing = jnp.take(state, send_order, axis=0).reshape((ndp, pair) + state.shape[1:])
    incoming = lax.all_to_all(outgoing, "dp", split_axis=0, concat_axis=0, tiled=True)
    sorted_pos = jnp.sort(assign.reshape(ndp, req_dp), axis=1)
    arrived = lax.dynamic_slice_in_dim(sorted_pos, dindex * pair, pair, 1) - dindex * req_dp
    slot_order = jnp.argsort(arrived.reshape(-1))
    return jnp.take(incoming.reshape(state.shape), slot_order, axis=0)


def on_device(
    prefill_state,
    assign,
    tokens,
    embed_table,
    w_xz,
    w_dt,
    w_bc,
    dt_bias,
    a_log,
    d_skip,
    norm_w,
    w_out,
):
    ntensor = lax.axis_size("tensor")
    ndp = lax.axis_size("dp")
    tindex = lax.axis_index("tensor")
    dindex = lax.axis_index("dp")
    req_dp, heads_dev, head_dim, state_dim = prefill_state.shape
    requests = req_dp * ndp
    steps = tokens.shape[1]
    quads = ntensor // RANKS
    group_req = req_dp // quads
    rank_heads = heads_dev // RANKS
    per_group = HEADS // GROUPS
    state_heads = to_groups(prefill_state, assign, dindex, ndp)
    inverse = jnp.argsort(assign)
    tok_pos = jnp.take(tokens, inverse, axis=0)
    vocab_dev = embed_table.shape[0]
    local_ids = tok_pos - tindex * vocab_dev
    inside = (local_ids >= 0) & (local_ids < vocab_dev)
    looked = jnp.take(embed_table, jnp.clip(local_ids, 0, vocab_dev - 1), axis=0)
    terms = jnp.where(inside[..., None], looked.astype(jnp.float32), 0.0)
    emb_mine = lax.psum_scatter(
        terms.astype(jnp.bfloat16), "tensor", scatter_dimension=0, tiled=True
    ).astype(jnp.float32)
    emb_all = lax.all_gather(emb_mine.astype(jnp.bfloat16), "tensor", axis=0, tiled=True)
    dmodel_dev = emb_all.shape[2]
    flat_emb = emb_all.reshape(requests * steps, dmodel_dev)
    xz_part = jnp.dot(
        flat_emb,
        w_xz.reshape(dmodel_dev, heads_dev * 2 * head_dim),
        preferred_element_type=jnp.float32,
    )
    xz_part = jnp.transpose(xz_part.reshape(requests, steps, heads_dev, 2 * head_dim), (0, 2, 1, 3))
    dt_part = jnp.dot(flat_emb, w_dt, preferred_element_type=jnp.float32)
    dt_part = jnp.transpose(dt_part.reshape(requests, steps, heads_dev), (0, 2, 1))
    bc_part = jnp.dot(flat_emb, w_bc, preferred_element_type=jnp.float32).reshape(
        requests, steps, w_bc.shape[1]
    )
    xz_heads, dt_heads, bc_heads = (
        lax.psum_scatter(xz_part, "dp", scatter_dimension=0, tiled=True),
        lax.psum_scatter(dt_part, "dp", scatter_dimension=0, tiled=True),
        lax.psum_scatter(bc_part, "dp", scatter_dimension=0, tiled=True),
    )
    bc_rows = lax.all_gather(bc_heads, "tensor", axis=2, tiled=True)
    state_quads = lax.all_to_all(
        arrange(state_heads, quads, RANKS), "tensor", split_axis=0, concat_axis=0, tiled=True
    )
    xz_quads, dt_quads = (
        lax.all_to_all(
            arrange(xz_heads, quads, RANKS), "tensor", split_axis=0, concat_axis=0, tiled=True
        ),
        lax.all_to_all(
            arrange(dt_heads, quads, RANKS), "tensor", split_axis=0, concat_axis=0, tiled=True
        ),
    )
    quad = tindex // RANKS
    rank = tindex % RANKS
    head_ids = (
        jnp.arange(ntensor)[:, None] * heads_dev
        + rank * rank_heads
        + jnp.arange(rank_heads)[None, :]
    )
    group_ids = head_ids // per_group
    all_bias, all_alog, all_skip, all_norm = (
        lax.all_gather(dt_bias, "tensor", axis=0, tiled=True),
        lax.all_gather(a_log, "tensor", axis=0, tiled=True),
        lax.all_gather(d_skip, "tensor", axis=0, tiled=True),
        lax.all_gather(norm_w, "tensor", axis=0, tiled=True),
    )

    def pick(values):
        shaped = values.reshape((ntensor, RANKS, rank_heads) + values.shape[1:])
        return lax.dynamic_index_in_dim(shaped, rank, 1, keepdims=False)

    bias_quad = pick(all_bias)[..., None]
    rate_quad = jnp.exp(pick(all_alog))[..., None]
    skip_quad = pick(all_skip)[..., None]
    norm_quad = pick(all_norm)
    my_rows = lax.dynamic_slice_in_dim(bc_rows, quad * group_req, group_req, 0).reshape(
        group_req, steps, GROUPS, 2 * state_dim
    )
    bc_quad = jnp.transpose(jnp.take(my_rows, group_ids, axis=2), (2, 3, 0, 1, 4))
    state_quads, gated = advance(
        state_quads, xz_quads, dt_quads, bc_quad, bias_quad, rate_quad, skip_quad
    )
    squares = jnp.sum(gated * gated, axis=-1)
    members = (group_ids[..., None] == jnp.arange(GROUPS)).astype(jnp.float32)
    grouped = jnp.einsum("tmjs,tmg->jsg", squares, members, precision=lax.Precision.HIGHEST)
    partial_value = lax.dynamic_update_slice_in_dim(
        jnp.zeros((req_dp, steps, GROUPS), jnp.float32), grouped, quad * group_req, 0
    )
    totals = group_totals(partial_value, RANKS.bit_length() - 1)
    mine_tot = lax.dynamic_slice_in_dim(totals, quad * group_req, group_req, 0)
    scale = lax.rsqrt(jnp.take(mine_tot, group_ids, axis=2) / (per_group * head_dim) + norm_eps)
    scale = jnp.transpose(scale, (2, 3, 0, 1))
    normed_quad = (gated * scale[..., None] * norm_quad[:, :, None, None, :]).astype(jnp.bfloat16)
    returned = lax.all_to_all(normed_quad, "tensor", split_axis=0, concat_axis=0, tiled=True)
    normed = restore(returned, quads, RANKS)
    decode_state = state_quads.reshape((1, 1, ntensor * rank_heads, group_req, head_dim, state_dim))
    mixed_in = jnp.transpose(normed, (0, 2, 1, 3)).reshape(req_dp, steps, heads_dev * head_dim)
    mix_all = jnp.einsum(
        "rsk,kd->rsd",
        lax.all_gather(mixed_in, "dp", axis=0, tiled=True),
        w_out,
        preferred_element_type=jnp.float32,
    )
    mix_mine = lax.psum_scatter(mix_all, "tensor", scatter_dimension=0, tiled=True)
    layer_out = (emb_mine + mix_mine).astype(jnp.bfloat16)
    return (layer_out, decode_state)


def lookup_kernel(assign, tokens, table, emb, idx, inv, buf, rows32, sems):
    d = lax.axis_index("dp")
    t = lax.axis_index("tensor")
    requests = assign.shape[0]
    vocab_dev = table.shape[0]
    req_dp = requests // lax.axis_size("dp")
    nrows = buf.shape[0]
    steps = tokens.shape[1]
    for i in range(requests):
        inv[assign[i]] = i
    for i in range(req_dp):
        idx[assign[d * req_dp + i] // req_dp] = i
    for k in range(req_dp):
        idx[req_dp + k] = inv[d * req_dp + k] // req_dp
    local, copies = [], []
    for row in range(nrows):
        loc = tokens[inv[row // steps], row % steps] - t * vocab_dev
        clipped = jnp.clip(loc, 0, vocab_dev - 1)
        base = pl.multiple_of((clipped // 16) * 16, 16)
        copy = pltpu.make_async_copy(table.at[pl.ds(base, 16), :], buf.at[row], sems.at[row])
        copy.start()
        copies.append(copy)
        local.append(jnp.where(loc == clipped, clipped - base, -1))
    sub = lax.broadcasted_iota(jnp.int32, (16, 1), 0)
    for row in range(nrows):
        copies[row].wait()
        picked = jnp.where(sub == local[row], buf[row].astype(jnp.float32), 0.0)
        rows32[row : row + 1, :] = jnp.sum(picked, axis=0, keepdims=True)
    width = emb.shape[2]
    for c in range(emb.shape[0]):
        emb[c] = rows32[:, c * width : (c + 1) * width].astype(jnp.bfloat16)


def split2(value):
    high = value.astype(jnp.bfloat16).astype(jnp.float32)
    return high, value - high


def layer_kernel(
    idx, embm, state, w_xz, w_bc, w_dt, bias, alog, skip, norm_w, w_out,
    lo_out, ds_out,
    state_v, wxz_v, wout_v, rsbuf, full, part, prx, snd1, arr0, arr1, arr2, arr3, stage, fin, sc, nall,
    mix32, own32, mo, mrx, pk, pkrx, ost,
    st_sem, w_sem, wo_sem, es_s, es_r, eg_s, eg_r, p1_s, p1_r, p2_s, p2_r,
    x_s, x_r, n_s, n_r, k_s, k_r, m_s, m_r, o_sem,
):
    f32, bf16 = jnp.float32, jnp.bfloat16
    d = lax.axis_index("dp")
    t = lax.axis_index("tensor")
    ND, NT = 4, 8
    arr = (arr0, arr1, arr2, arr3)

    def remote(src, dst, send, recv, axis, peer):
        return pltpu.make_async_remote_copy(
            src_ref=src, dst_ref=dst, send_sem=send, recv_sem=recv,
            device_id={axis: peer}, device_id_type=pl.DeviceIdType.MESH,
        )

    st_copy = pltpu.make_async_copy(state, state_v, st_sem.at[0])
    st_copy.start()

    def w_copy(k):
        rows = pl.ds(pl.multiple_of(k * 256, 256), 256)
        return pltpu.make_async_copy(w_xz.at[rows], wxz_v.at[rows], w_sem.at[k])

    for k in range(8):
        w_copy(k).start()
    wo_copy = pltpu.make_async_copy(w_out, wout_v, wo_sem.at[0])
    wo_copy.start()

    barrier = pltpu.get_barrier_semaphore()
    for o in range(1, ND):
        pl.semaphore_signal(barrier, inc=1, device_id={"dp": lax.rem(d + o, ND)},
                            device_id_type=pl.DeviceIdType.MESH)
    for o in range(1, NT):
        pl.semaphore_signal(barrier, inc=1, device_id={"tensor": lax.rem(t + o, NT)},
                            device_id_type=pl.DeviceIdType.MESH)
    pl.semaphore_wait(barrier, ND + NT - 2)

    sent = []
    es = []
    for o in range(1, NT):
        peer = lax.rem(t + o, NT)
        c = remote(embm.at[peer], rsbuf.at[o], es_s.at[o], es_r.at[o], "tensor", peer)
        c.start()
        es.append(c)
    sent += es

    st_copy.wait()
    p1 = []

    def send_chunk(m):
        r = lax.rem(t + m, 4)
        copies = []
        for o in range(1, ND):
            peer = lax.rem(d + o, ND)
            snd1[peer, r] = state_v[idx[peer], r].astype(bf16)
            c = remote(snd1.at[peer, r], arr[m].at[d], p1_s.at[m, o], p1_r.at[m, o], "dp", peer)
            c.start()
            copies.append(c)
        arr[m][d] = state_v[idx[d], r].astype(bf16)
        return copies

    p1.append(send_chunk(0))
    for c in es:
        c.wait_recv()
    total = embm[t].astype(f32)
    for o in range(1, NT):
        total = total + rsbuf[o].astype(f32)
    full[t] = total.astype(bf16)
    eg = []
    for o in range(1, NT):
        peer = lax.rem(t + o, NT)
        c = remote(full.at[t], full.at[t], eg_s.at[o], eg_r.at[o], "tensor", peer)
        c.start()
        eg.append(c)
    sent += eg
    for m in range(1, 4):
        p1.append(send_chunk(m))
    for copies in p1:
        sent += copies
    for c in eg:
        c.wait_recv()

    def forward(m):
        r = lax.rem(t + m, 4)
        for c in p1[m]:
            c.wait_recv()
        for k in range(4):
            stage[r, k] = arr[m][idx[4 + k]]
        out = []
        for o in (m, m + 4):
            peer = lax.rem(t + o, NT)
            first = pl.multiple_of((peer // 4) * 2, 2)
            if o == 0:
                for j in range(2):
                    fin[0, j] = stage[r, first + j]
                continue
            c = remote(stage.at[r, pl.ds(first, 2)], fin.at[o], p2_s.at[o], p2_r.at[o], "tensor", peer)
            c.start()
            out.append((o, c))
        return out

    part[:, :, 4352:4480] = jnp.zeros((4, 8, 128), f32)
    p2 = {}
    for m in range(4):
        for k in (2 * m, 2 * m + 1):
            w_copy(k).wait()
            e = full[k]
            swapped = jnp.swapaxes(wxz_v[k * 256 : (k + 1) * 256], 0, 1)

            def add(lo, width, value, first=(k == 0)):
                value = value.reshape(4, 8, width)
                if first and lo < 4352:
                    part[:, :, lo : lo + width] = value
                else:
                    part[:, :, lo : lo + width] += value

            for h in range(32):
                add(h * 128, 128, jnp.dot(e, swapped[h], preferred_element_type=f32))
            add(4096, 256, jnp.dot(e, w_bc[k * 256 : (k + 1) * 256, :], preferred_element_type=f32))
            add(4352, 32, jnp.dot(e, w_dt[k * 256 : (k + 1) * 256, :], preferred_element_type=f32))
        p2.update(dict(forward(m)))
    sent += list(p2.values())

    xs = []
    for o in range(1, ND):
        peer = lax.rem(d + o, ND)
        c = remote(part.at[peer], prx.at[o], x_s.at[o], x_r.at[o], "dp", peer)
        c.start()
        xs.append(c)
    sent += xs
    for c in xs:
        c.wait_recv()
    proj = part[d] + prx[1] + prx[2] + prx[3]

    low = lax.broadcasted_iota(jnp.int32, (8, 128), 1) < 64
    xt, zt = [], []
    for k in range(16):
        a = proj[:, k * 256 : k * 256 + 128]
        b = proj[:, k * 256 + 128 : k * 256 + 256]
        xt.append(jnp.where(low, a, pltpu.roll(b, 64, 1)))
        zt.append(jnp.where(low, pltpu.roll(a, 64, 1), b))
    x = jnp.concatenate(xt, axis=1)
    z = jnp.concatenate(zt, axis=1)
    bc = proj[:, 4096:4352]
    raw = proj[:, 4352:4384] + bias[...]
    delta = jnp.maximum(raw, 0.0) + jnp.log1p(jnp.exp(-jnp.abs(raw)))
    decay = jnp.exp(-delta * jnp.exp(alog[...]))
    head_of = lax.broadcasted_iota(jnp.int32, (32, 2048), 1) // 64
    spread = (head_of == lax.broadcasted_iota(jnp.int32, (32, 2048), 0)).astype(f32)
    per_head = jnp.concatenate([delta, decay, jnp.broadcast_to(skip[...], (8, 32))], axis=0)
    per_lane = jnp.dot(per_head, spread, precision=lax.Precision.HIGHEST, preferred_element_type=f32)

    def step(value, s):
        return jnp.concatenate([value[2 * k + s : 2 * k + s + 1] for k in range(4)], axis=0)

    dx = per_lane[0:8] * x
    x0, x1, z0, z1 = step(x, 0), step(x, 1), step(z, 0), step(z, 1)
    u0, u1 = step(dx, 0), step(dx, 1)
    a0, a1 = step(per_lane[8:16], 0), step(per_lane[8:16], 1)
    sk = per_lane[16:20]
    b0, b1 = step(bc[:, :128], 0), step(bc[:, :128], 1)
    c0, c1 = step(bc[:, 128:], 0), step(bc[:, 128:], 1)
    c0h, c0l = split2(c0)
    c1h, c1l = split2(c1)
    pad12 = jnp.zeros((12, 128), f32)
    for k in range(4):
        rows = [v[k : k + 1] for v in (c0h, c0l, c1h, c1l)]
        cmat = jnp.concatenate(rows + [pad12], axis=0).astype(bf16)
        for r in range(4):
            prod = lax.dot_general(cmat, stage[r, k], (((1,), (1,)), ((), ())), preferred_element_type=f32)
            sc[0, k : k + 1, r * 512 : (r + 1) * 512] = prod[0:1] + prod[1:2]
            sc[1, k : k + 1, r * 512 : (r + 1) * 512] = prod[2:3] + prod[3:4]
    b0c0 = jnp.sum(b0 * c0, axis=1, keepdims=True)
    b0c1 = jnp.sum(b0 * c1, axis=1, keepdims=True)
    b1c1 = jnp.sum(b1 * c1, axis=1, keepdims=True)
    y0 = a0 * sc[0, 0:4, :] + u0 * b0c0 + sk * x0
    y1 = a1 * (a0 * sc[1, 0:4, :] + u0 * b0c1) + u1 * b1c1 + sk * x1
    g0 = y0 * (z0 * (1.0 / (1.0 + jnp.exp(-z0))))
    g1 = y1 * (z1 * (1.0 / (1.0 + jnp.exp(-z1))))
    width = g0.shape[1]

    def norm(g):
        ms = jnp.sum(g * g, axis=1, keepdims=True) / width
        return g * lax.rsqrt(ms + norm_eps) * norm_w[...]

    n0, n1 = norm(g0), norm(g1)
    normed = jnp.concatenate([v[k : k + 1] for k in range(4) for v in (n0, n1)], axis=0)
    nall[d] = jnp.concatenate([normed[:, :1024], normed[:, 1024:]], axis=0).astype(bf16)
    ns = []
    for o in range(1, ND):
        peer = lax.rem(d + o, ND)
        c = remote(nall.at[d], nall.at[d], n_s.at[o], n_r.at[o], "dp", peer)
        c.start()
        ns.append(c)
    sent += ns

    aa = a0 * a1
    v0 = a1 * u0
    pad256 = jnp.zeros((4, 256), f32)
    bb = jnp.concatenate([b0, b1, pad256], axis=1)
    for c in range(NT):
        q, r = c // 4, c % 4
        rows = []
        for j in range(2):
            k = 2 * q + j
            for v in (v0, u1, aa):
                rows.append(v[k : k + 1, r * 512 : (r + 1) * 512])
            rows.append(bb[k : k + 1])
        pk[c] = jnp.concatenate(rows, axis=0)
    ks = {}
    for o in range(1, NT):
        peer = lax.rem(t + o, NT)
        c = remote(pk.at[peer], pkrx.at[o], k_s.at[o], k_r.at[o], "tensor", peer)
        c.start()
        ks[o] = c
    sent += list(ks.values())

    for c in ns:
        c.wait_recv()
    blocks = []
    for s in range(ND):
        v = nall[s].astype(f32)
        blocks.append(jnp.concatenate([v[0:8], v[8:16]], axis=1))
    nmat = jnp.concatenate(blocks, axis=0).astype(bf16)
    wo_copy.wait()
    for q in range(4):
        mix = jnp.dot(nmat, wout_v[:, q * 512 : (q + 1) * 512], preferred_element_type=f32)
        emb = jnp.concatenate([full[2 * q], full[2 * q + 1]], axis=1).astype(f32)
        mixed = mix + emb
        for c in range(NT):
            mix32[c, 4 * q : 4 * q + 4, :] = mix[4 * c : 4 * c + 4]
            own32[c, 4 * q : 4 * q + 4, :] = mixed[4 * c : 4 * c + 4]
    for c in range(NT):
        mo[c] = mix32[c].astype(bf16)
    ms = []
    for o in range(1, NT):
        peer = lax.rem(t + o, NT)
        c = remote(mo.at[peer], mrx.at[o], m_s.at[o], m_r.at[o], "tensor", peer)
        c.start()
        ms.append(c)
    sent += ms

    def finish(o):
        source = lax.rem(t + NT - o, NT)
        if o == 0:
            pack = pk[t]
        else:
            p2[o].wait_recv()
            ks[o].wait_recv()
            pack = pkrx[o]
        for j in range(2):
            uh, ul = split2(pack[4 * j : 4 * j + 1])
            wh, wl = split2(pack[4 * j + 1 : 4 * j + 2])
            ah, al = split2(pack[4 * j + 2 : 4 * j + 3])
            bh, bl = split2(pack[4 * j + 3 : 4 * j + 4])
            left = jnp.concatenate(
                [uh, uh, ul, wh, wh, wl, ah, al, jnp.zeros((8, 512), f32)], axis=0
            ).astype(bf16)
            b0h, b0l, b1h, b1l = bh[:, :128], bl[:, :128], bh[:, 128:256], bl[:, 128:256]
            outer = jnp.concatenate(
                [b0h, b0l, b0h, b1h, b1l, b1h, jnp.zeros((10, 128), f32)], axis=0
            ).astype(bf16)
            row = lax.broadcasted_iota(jnp.int32, (16, 128), 0)
            ones = jnp.where((row == 6) | (row == 7), 1.0, 0.0).astype(bf16)
            right = jnp.concatenate([ones, outer], axis=1)
            g = lax.dot_general(left, right, (((0,), (0,)), ((), ())), preferred_element_type=f32)
            new = fin[o, j].astype(f32) * g[:, :128] + g[:, 128:]
            ost[o, :, j] = new.reshape(8, 64, 128)
        c = pltpu.make_async_copy(ost.at[o], ds_out.at[source], o_sem.at[o])
        c.start()
        return c

    outs = [finish(0)]
    for c in ms:
        c.wait_recv()
    own = own32[t]
    for o in range(1, NT):
        own = own + mrx[o].astype(f32)
    lo_out[...] = jnp.concatenate([own[4 * q : 4 * q + 4] for q in range(4)], axis=1).astype(bf16)
    for o in (4, 1, 5, 2, 6, 3, 7):
        outs.append(finish(o))
    for c in sent:
        c.wait_send()
    for c in outs:
        c.wait()


def fused(
    prefill_state, assign, tokens, embed_table, w_xz, w_dt, w_bc, dt_bias, a_log, d_skip, norm_w, w_out
):
    f32, bf16 = jnp.float32, jnp.bfloat16
    vmem = pl.BlockSpec(memory_space=pltpu.VMEM)
    smem = pl.BlockSpec(memory_space=pltpu.SMEM)
    hbm = pl.BlockSpec(memory_space=pl.ANY)
    embm, idx = pl.pallas_call(
        lookup_kernel,
        out_shape=(
            jax.ShapeDtypeStruct((8, 32, 256), bf16),
            jax.ShapeDtypeStruct((8,), jnp.int32),
        ),
        in_specs=[smem, smem, hbm],
        out_specs=(vmem, smem),
        scratch_shapes=[
            pltpu.SMEM((16,), jnp.int32),
            pltpu.VMEM((32, 16, 2048), bf16),
            pltpu.VMEM((32, 2048), f32),
            pltpu.SemaphoreType.DMA((32,)),
        ],
        compiler_params=pltpu.CompilerParams(vmem_limit_bytes=8 << 20),
    )(assign, tokens, embed_table)
    dma = pltpu.SemaphoreType.DMA
    layer_out, decode_state = pl.pallas_call(
        layer_kernel,
        out_shape=(
            jax.ShapeDtypeStruct((4, 2048), bf16),
            jax.ShapeDtypeStruct((8, 8, 2, 64, 128), f32),
        ),
        in_specs=[smem, vmem, hbm, hbm, vmem, vmem, vmem, vmem, vmem, vmem, hbm],
        out_specs=(vmem, hbm),
        scratch_shapes=[
            pltpu.VMEM((4, 4, 512, 128), f32),
            pltpu.VMEM((2048, 32, 128), bf16),
            pltpu.VMEM((2048, 2048), bf16),
            pltpu.VMEM((8, 32, 256), bf16),
            pltpu.VMEM((8, 32, 256), bf16),
            pltpu.VMEM((4, 8, 4480), f32),
            pltpu.VMEM((4, 8, 4480), f32),
            pltpu.VMEM((4, 4, 512, 128), bf16),
            pltpu.VMEM((4, 512, 128), bf16),
            pltpu.VMEM((4, 512, 128), bf16),
            pltpu.VMEM((4, 512, 128), bf16),
            pltpu.VMEM((4, 512, 128), bf16),
            pltpu.VMEM((4, 4, 512, 128), bf16),
            pltpu.VMEM((8, 2, 512, 128), bf16),
            pltpu.VMEM((2, 8, 2048), f32),
            pltpu.VMEM((4, 16, 1024), bf16),
            pltpu.VMEM((8, 16, 512), f32),
            pltpu.VMEM((8, 16, 512), f32),
            pltpu.VMEM((8, 16, 512), bf16),
            pltpu.VMEM((8, 16, 512), bf16),
            pltpu.VMEM((8, 8, 512), f32),
            pltpu.VMEM((8, 8, 512), f32),
            pltpu.VMEM((8, 8, 2, 64, 128), f32),
            dma((1,)), dma((8,)), dma((1,)),
            dma((8,)), dma((8,)), dma((8,)), dma((8,)),
            dma((4, 4)), dma((4, 4)), dma((8,)), dma((8,)),
            dma((4,)), dma((4,)), dma((4,)), dma((4,)),
            dma((8,)), dma((8,)), dma((8,)), dma((8,)), dma((8,)),
        ],
        compiler_params=pltpu.CompilerParams(
            collective_id=0, has_side_effects=True, vmem_limit_bytes=60 << 20
        ),
        cost_estimate=pl.CostEstimate(
            flops=900_000_000, bytes_accessed=40_000_000, transcendentals=100_000
        ),
    )(
        idx, embm, prefill_state.reshape(4, 4, 512, 128), w_xz, w_bc, w_dt,
        dt_bias.reshape(1, 32), a_log.reshape(1, 32), d_skip.reshape(1, 32),
        norm_w.reshape(1, 2048), w_out,
    )
    return layer_out.reshape(2, 2, 2048), decode_state.reshape(1, 1, 64, 2, 64, 128)


def solution(mesh):
    sizes = (mesh.shape["dp"], mesh.shape["tensor"])
    in_specs = (
        P("dp", "tensor", None, None),
        P(),
        P(),
        P("tensor", "dp"),
        P("dp", "tensor", None),
        P("dp", "tensor"),
        P("dp", "tensor"),
        P("tensor"),
        P("tensor"),
        P("tensor"),
        P("tensor", None),
        P("tensor", "dp"),
    )
    out_specs = (P("tensor", None, "dp"), P("dp", "tensor", None, None, None, None))
    return jax.shard_map(
        fused if sizes == (4, 8) else on_device, mesh=mesh, in_specs=in_specs, out_specs=out_specs, check_vma=False
    )
```

```python
import jax
import jax.numpy as jnp
from jax import lax
from jax.experimental import pallas as pl
from jax.experimental.pallas import tpu as pltpu
from jax.sharding import PartitionSpec as P

HEADS = 256
GROUPS = 8
RANKS = 4


norm_eps = 1e-05


def partner(value, axis, apart):
    mask = 2**apart
    pairs = [(source, source ^ mask) for source in range(lax.axis_size(axis))]
    return lax.ppermute(value, axis, pairs)


def arrange(value, quads, ranks):
    rest = value.shape[2:]
    group_req = value.shape[0] // quads
    rank_heads = value.shape[1] // ranks
    shaped = value.reshape((quads, group_req, ranks, rank_heads) + rest)
    extra = tuple(range(4, 4 + len(rest)))
    moved = jnp.transpose(shaped, (0, 2, 3, 1) + extra)
    return moved.reshape((quads * ranks, rank_heads, group_req) + rest)


def restore(value, quads, ranks):
    rank_heads = value.shape[1]
    group_req = value.shape[2]
    rest = value.shape[3:]
    shaped = value.reshape((quads, ranks, rank_heads, group_req) + rest)
    extra = tuple(range(4, 4 + len(rest)))
    moved = jnp.transpose(shaped, (0, 3, 1, 2) + extra)
    return moved.reshape((quads * group_req, ranks * rank_heads) + rest)


def advance(ssm_state, inputs, raw_dt, bc_rows, bias, decay_rate, skip):
    steps = raw_dt.shape[-1]
    head_dim = inputs.shape[-1] // 2
    state_dim = bc_rows.shape[-1] // 2
    results = []
    for step_idx in range(steps):
        xin = inputs[..., step_idx, :head_dim]
        zin = inputs[..., step_idx, head_dim:]
        bvec = bc_rows[..., step_idx, :state_dim]
        cvec = bc_rows[..., step_idx, state_dim:]
        delta = jax.nn.softplus(raw_dt[..., step_idx] + bias)
        decay = jnp.exp(-delta * decay_rate)
        ssm_state = (
            ssm_state * decay[..., None, None]
            + (delta[..., None] * xin)[..., :, None] * bvec[..., None, :]
        )
        yout = jnp.sum(ssm_state * cvec[..., None, :], axis=-1) + skip[..., None] * xin
        results.append(yout * jax.nn.silu(zin))
    return (ssm_state, jnp.stack(results, axis=-2))


def group_totals(partial_value, bit_count):
    for bit in range(bit_count):
        partial_value = partial_value + partner(partial_value, "tensor", bit)
    return partial_value


def to_groups(state, assign, dindex, ndp):
    req_dp = state.shape[0]
    pair = req_dp // ndp
    own_pos = lax.dynamic_slice_in_dim(assign, dindex * req_dp, req_dp)
    send_order = jnp.argsort(own_pos)
    outgoing = jnp.take(state, send_order, axis=0).reshape((ndp, pair) + state.shape[1:])
    incoming = lax.all_to_all(outgoing, "dp", split_axis=0, concat_axis=0, tiled=True)
    sorted_pos = jnp.sort(assign.reshape(ndp, req_dp), axis=1)
    arrived = lax.dynamic_slice_in_dim(sorted_pos, dindex * pair, pair, 1) - dindex * req_dp
    slot_order = jnp.argsort(arrived.reshape(-1))
    return jnp.take(incoming.reshape(state.shape), slot_order, axis=0)


def on_device(
    prefill_state,
    assign,
    tokens,
    embed_table,
    w_xz,
    w_dt,
    w_bc,
    dt_bias,
    a_log,
    d_skip,
    norm_w,
    w_out,
):
    ntensor = lax.axis_size("tensor")
    ndp = lax.axis_size("dp")
    tindex = lax.axis_index("tensor")
    dindex = lax.axis_index("dp")
    req_dp, heads_dev, head_dim, state_dim = prefill_state.shape
    requests = req_dp * ndp
    steps = tokens.shape[1]
    quads = ntensor // RANKS
    group_req = req_dp // quads
    rank_heads = heads_dev // RANKS
    per_group = HEADS // GROUPS
    state_heads = to_groups(prefill_state, assign, dindex, ndp)
    inverse = jnp.argsort(assign)
    tok_pos = jnp.take(tokens, inverse, axis=0)
    vocab_dev = embed_table.shape[0]
    local_ids = tok_pos - tindex * vocab_dev
    inside = (local_ids >= 0) & (local_ids < vocab_dev)
    looked = jnp.take(embed_table, jnp.clip(local_ids, 0, vocab_dev - 1), axis=0)
    terms = jnp.where(inside[..., None], looked.astype(jnp.float32), 0.0)
    emb_mine = lax.psum_scatter(
        terms.astype(jnp.bfloat16), "tensor", scatter_dimension=0, tiled=True
    ).astype(jnp.float32)
    emb_all = lax.all_gather(emb_mine.astype(jnp.bfloat16), "tensor", axis=0, tiled=True)
    dmodel_dev = emb_all.shape[2]
    flat_emb = emb_all.reshape(requests * steps, dmodel_dev)
    xz_part = jnp.dot(
        flat_emb,
        w_xz.reshape(dmodel_dev, heads_dev * 2 * head_dim),
        preferred_element_type=jnp.float32,
    )
    xz_part = jnp.transpose(xz_part.reshape(requests, steps, heads_dev, 2 * head_dim), (0, 2, 1, 3))
    dt_part = jnp.dot(flat_emb, w_dt, preferred_element_type=jnp.float32)
    dt_part = jnp.transpose(dt_part.reshape(requests, steps, heads_dev), (0, 2, 1))
    bc_part = jnp.dot(flat_emb, w_bc, preferred_element_type=jnp.float32).reshape(
        requests, steps, w_bc.shape[1]
    )
    xz_heads, dt_heads, bc_heads = (
        lax.psum_scatter(xz_part, "dp", scatter_dimension=0, tiled=True),
        lax.psum_scatter(dt_part, "dp", scatter_dimension=0, tiled=True),
        lax.psum_scatter(bc_part, "dp", scatter_dimension=0, tiled=True),
    )
    bc_rows = lax.all_gather(bc_heads, "tensor", axis=2, tiled=True)
    state_quads = lax.all_to_all(
        arrange(state_heads, quads, RANKS), "tensor", split_axis=0, concat_axis=0, tiled=True
    )
    xz_quads, dt_quads = (
        lax.all_to_all(
            arrange(xz_heads, quads, RANKS), "tensor", split_axis=0, concat_axis=0, tiled=True
        ),
        lax.all_to_all(
            arrange(dt_heads, quads, RANKS), "tensor", split_axis=0, concat_axis=0, tiled=True
        ),
    )
    quad = tindex // RANKS
    rank = tindex % RANKS
    head_ids = (
        jnp.arange(ntensor)[:, None] * heads_dev
        + rank * rank_heads
        + jnp.arange(rank_heads)[None, :]
    )
    group_ids = head_ids // per_group
    all_bias, all_alog, all_skip, all_norm = (
        lax.all_gather(dt_bias, "tensor", axis=0, tiled=True),
        lax.all_gather(a_log, "tensor", axis=0, tiled=True),
        lax.all_gather(d_skip, "tensor", axis=0, tiled=True),
        lax.all_gather(norm_w, "tensor", axis=0, tiled=True),
    )

    def pick(values):
        shaped = values.reshape((ntensor, RANKS, rank_heads) + values.shape[1:])
        return lax.dynamic_index_in_dim(shaped, rank, 1, keepdims=False)

    bias_quad = pick(all_bias)[..., None]
    rate_quad = jnp.exp(pick(all_alog))[..., None]
    skip_quad = pick(all_skip)[..., None]
    norm_quad = pick(all_norm)
    my_rows = lax.dynamic_slice_in_dim(bc_rows, quad * group_req, group_req, 0).reshape(
        group_req, steps, GROUPS, 2 * state_dim
    )
    bc_quad = jnp.transpose(jnp.take(my_rows, group_ids, axis=2), (2, 3, 0, 1, 4))
    state_quads, gated = advance(
        state_quads, xz_quads, dt_quads, bc_quad, bias_quad, rate_quad, skip_quad
    )
    squares = jnp.sum(gated * gated, axis=-1)
    members = (group_ids[..., None] == jnp.arange(GROUPS)).astype(jnp.float32)
    grouped = jnp.einsum("tmjs,tmg->jsg", squares, members, precision=lax.Precision.HIGHEST)
    partial_value = lax.dynamic_update_slice_in_dim(
        jnp.zeros((req_dp, steps, GROUPS), jnp.float32), grouped, quad * group_req, 0
    )
    totals = group_totals(partial_value, RANKS.bit_length() - 1)
    mine_tot = lax.dynamic_slice_in_dim(totals, quad * group_req, group_req, 0)
    scale = lax.rsqrt(jnp.take(mine_tot, group_ids, axis=2) / (per_group * head_dim) + norm_eps)
    scale = jnp.transpose(scale, (2, 3, 0, 1))
    normed_quad = (gated * scale[..., None] * norm_quad[:, :, None, None, :]).astype(jnp.bfloat16)
    returned = lax.all_to_all(normed_quad, "tensor", split_axis=0, concat_axis=0, tiled=True)
    normed = restore(returned, quads, RANKS)
    decode_state = state_quads.reshape((1, 1, ntensor * rank_heads, group_req, head_dim, state_dim))
    mixed_in = jnp.transpose(normed, (0, 2, 1, 3)).reshape(req_dp, steps, heads_dev * head_dim)
    mix_all = jnp.einsum(
        "rsk,kd->rsd",
        lax.all_gather(mixed_in, "dp", axis=0, tiled=True),
        w_out,
        preferred_element_type=jnp.float32,
    )
    mix_mine = lax.psum_scatter(mix_all, "tensor", scatter_dimension=0, tiled=True)
    layer_out = (emb_mine + mix_mine).astype(jnp.bfloat16)
    return (layer_out, decode_state)


def lookup_kernel(assign, tokens, table, emb, idx, inv, buf, rows32, sems):
    d = lax.axis_index("dp")
    t = lax.axis_index("tensor")
    requests = assign.shape[0]
    vocab_dev = table.shape[0]
    req_dp = requests // lax.axis_size("dp")
    nrows = buf.shape[0]
    steps = tokens.shape[1]
    for i in range(requests):
        inv[assign[i]] = i
    for i in range(req_dp):
        idx[assign[d * req_dp + i] // req_dp] = i
    for k in range(req_dp):
        idx[req_dp + k] = inv[d * req_dp + k] // req_dp
    local, copies = [], []
    for row in range(nrows):
        loc = tokens[inv[row // steps], row % steps] - t * vocab_dev
        clipped = jnp.clip(loc, 0, vocab_dev - 1)
        base = pl.multiple_of((clipped // 16) * 16, 16)
        copy = pltpu.make_async_copy(table.at[pl.ds(base, 16), :], buf.at[row], sems.at[row])
        copy.start()
        copies.append(copy)
        local.append(jnp.where(loc == clipped, clipped - base, -1))
    sub = lax.broadcasted_iota(jnp.int32, (16, 1), 0)
    for row in range(nrows):
        copies[row].wait()
        picked = jnp.where(sub == local[row], buf[row].astype(jnp.float32), 0.0)
        rows32[row : row + 1, :] = jnp.sum(picked, axis=0, keepdims=True)
    width = emb.shape[2]
    for c in range(emb.shape[0]):
        emb[c] = rows32[:, c * width : (c + 1) * width].astype(jnp.bfloat16)


def split2(value):
    high = value.astype(jnp.bfloat16).astype(jnp.float32)
    return high, value - high


def layer_kernel(
    idx, embm, state, w_xz, w_bc, w_dt, bias, alog, skip, norm_w, w_out,
    lo_out, ds_out,
    state_v, wxz_v, wout_v, rsbuf, full, part, prx, snd1, arr0, arr1, arr2, arr3, stage, fin, sc, nall,
    mix32, own32, mo, mrx, pk, pkrx, ost,
    st_sem, w_sem, wo_sem, es_s, es_r, eg_s, eg_r, p1_s, p1_r, p2_s, p2_r,
    x_s, x_r, n_s, n_r, k_s, k_r, m_s, m_r, o_sem,
):
    f32, bf16 = jnp.float32, jnp.bfloat16
    d = lax.axis_index("dp")
    t = lax.axis_index("tensor")
    ND, NT = 4, 8
    arr = (arr0, arr1, arr2, arr3)

    def remote(src, dst, send, recv, axis, peer):
        return pltpu.make_async_remote_copy(
            src_ref=src, dst_ref=dst, send_sem=send, recv_sem=recv,
            device_id={axis: peer}, device_id_type=pl.DeviceIdType.MESH,
        )

    st_copy = pltpu.make_async_copy(state, state_v, st_sem.at[0])
    st_copy.start()

    def w_copy(k):
        rows = pl.ds(pl.multiple_of(k * 256, 256), 256)
        return pltpu.make_async_copy(w_xz.at[rows], wxz_v.at[rows], w_sem.at[k])

    for k in range(8):
        w_copy(k).start()
    wo_copy = pltpu.make_async_copy(w_out, wout_v, wo_sem.at[0])
    wo_copy.start()

    barrier = pltpu.get_barrier_semaphore()
    for o in range(1, ND):
        pl.semaphore_signal(barrier, inc=1, device_id={"dp": lax.rem(d + o, ND)},
                            device_id_type=pl.DeviceIdType.MESH)
    for o in range(1, NT):
        pl.semaphore_signal(barrier, inc=1, device_id={"tensor": lax.rem(t + o, NT)},
                            device_id_type=pl.DeviceIdType.MESH)
    pl.semaphore_wait(barrier, ND + NT - 2)

    sent = []
    es = []
    for o in range(1, NT):
        peer = lax.rem(t + o, NT)
        c = remote(embm.at[peer], rsbuf.at[o], es_s.at[o], es_r.at[o], "tensor", peer)
        c.start()
        es.append(c)
    sent += es

    st_copy.wait()
    p1 = []

    def send_chunk(m):
        r = lax.rem(t + m, 4)
        copies = []
        for o in range(1, ND):
            peer = lax.rem(d + o, ND)
            snd1[peer, r] = state_v[idx[peer], r].astype(bf16)
            c = remote(snd1.at[peer, r], arr[m].at[d], p1_s.at[m, o], p1_r.at[m, o], "dp", peer)
            c.start()
            copies.append(c)
        arr[m][d] = state_v[idx[d], r].astype(bf16)
        return copies

    p1.append(send_chunk(0))
    for c in es:
        c.wait_recv()
    total = embm[t].astype(f32)
    for o in range(1, NT):
        total = total + rsbuf[o].astype(f32)
    full[t] = total.astype(bf16)
    eg = []
    for o in range(1, NT):
        peer = lax.rem(t + o, NT)
        c = remote(full.at[t], full.at[t], eg_s.at[o], eg_r.at[o], "tensor", peer)
        c.start()
        eg.append(c)
    sent += eg
    for m in range(1, 4):
        p1.append(send_chunk(m))
    for copies in p1:
        sent += copies
    for c in eg:
        c.wait_recv()

    def forward(m):
        r = lax.rem(t + m, 4)
        for c in p1[m]:
            c.wait_recv()
        for k in range(4):
            stage[r, k] = arr[m][idx[4 + k]]
        out = []
        for o in (m, m + 4):
            peer = lax.rem(t + o, NT)
            first = pl.multiple_of((peer // 4) * 2, 2)
            if o == 0:
                for j in range(2):
                    fin[0, j] = stage[r, first + j]
                continue
            c = remote(stage.at[r, pl.ds(first, 2)], fin.at[o], p2_s.at[o], p2_r.at[o], "tensor", peer)
            c.start()
            out.append((o, c))
        return out

    part[:, :, 4352:4480] = jnp.zeros((4, 8, 128), f32)
    p2 = {}
    for m in range(4):
        for k in (2 * m, 2 * m + 1):
            w_copy(k).wait()
            e = full[k]
            swapped = jnp.swapaxes(wxz_v[k * 256 : (k + 1) * 256], 0, 1)

            def add(lo, width, value, first=(k == 0)):
                value = value.reshape(4, 8, width)
                if first and lo < 4352:
                    part[:, :, lo : lo + width] = value
                else:
                    part[:, :, lo : lo + width] += value

            for h in range(32):
                add(h * 128, 128, jnp.dot(e, swapped[h], preferred_element_type=f32))
            add(4096, 256, jnp.dot(e, w_bc[k * 256 : (k + 1) * 256, :], preferred_element_type=f32))
            add(4352, 32, jnp.dot(e, w_dt[k * 256 : (k + 1) * 256, :], preferred_element_type=f32))
        p2.update(dict(forward(m)))
    sent += list(p2.values())

    xs = []
    for o in range(1, ND):
        peer = lax.rem(d + o, ND)
        c = remote(part.at[peer], prx.at[o], x_s.at[o], x_r.at[o], "dp", peer)
        c.start()
        xs.append(c)
    sent += xs
    for c in xs:
        c.wait_recv()
    proj = part[d] + prx[1] + prx[2] + prx[3]

    low = lax.broadcasted_iota(jnp.int32, (8, 128), 1) < 64
    xt, zt = [], []
    for k in range(16):
        a = proj[:, k * 256 : k * 256 + 128]
        b = proj[:, k * 256 + 128 : k * 256 + 256]
        xt.append(jnp.where(low, a, pltpu.roll(b, 64, 1)))
        zt.append(jnp.where(low, pltpu.roll(a, 64, 1), b))
    x = jnp.concatenate(xt, axis=1)
    z = jnp.concatenate(zt, axis=1)
    bc = proj[:, 4096:4352]
    raw = proj[:, 4352:4384] + bias[...]
    delta = jnp.maximum(raw, 0.0) + jnp.log1p(jnp.exp(-jnp.abs(raw)))
    decay = jnp.exp(-delta * jnp.exp(alog[...]))
    head_of = lax.broadcasted_iota(jnp.int32, (32, 2048), 1) // 64
    spread = (head_of == lax.broadcasted_iota(jnp.int32, (32, 2048), 0)).astype(f32)
    per_head = jnp.concatenate([delta, decay, jnp.broadcast_to(skip[...], (8, 32))], axis=0)
    per_lane = jnp.dot(per_head, spread, precision=lax.Precision.HIGHEST, preferred_element_type=f32)

    def step(value, s):
        return jnp.concatenate([value[2 * k + s : 2 * k + s + 1] for k in range(4)], axis=0)

    dx = per_lane[0:8] * x
    x0, x1, z0, z1 = step(x, 0), step(x, 1), step(z, 0), step(z, 1)
    u0, u1 = step(dx, 0), step(dx, 1)
    a0, a1 = step(per_lane[8:16], 0), step(per_lane[8:16], 1)
    sk = per_lane[16:20]
    b0, b1 = step(bc[:, :128], 0), step(bc[:, :128], 1)
    c0, c1 = step(bc[:, 128:], 0), step(bc[:, 128:], 1)
    c0h, c0l = split2(c0)
    c1h, c1l = split2(c1)
    pad12 = jnp.zeros((12, 128), f32)
    for k in range(4):
        rows = [v[k : k + 1] for v in (c0h, c0l, c1h, c1l)]
        cmat = jnp.concatenate(rows + [pad12], axis=0).astype(bf16)
        for r in range(4):
            prod = lax.dot_general(cmat, stage[r, k], (((1,), (1,)), ((), ())), preferred_element_type=f32)
            sc[0, k : k + 1, r * 512 : (r + 1) * 512] = prod[0:1] + prod[1:2]
            sc[1, k : k + 1, r * 512 : (r + 1) * 512] = prod[2:3] + prod[3:4]
    b0c0 = jnp.sum(b0 * c0, axis=1, keepdims=True)
    b0c1 = jnp.sum(b0 * c1, axis=1, keepdims=True)
    b1c1 = jnp.sum(b1 * c1, axis=1, keepdims=True)
    y0 = a0 * sc[0, 0:4, :] + u0 * b0c0 + sk * x0
    y1 = a1 * (a0 * sc[1, 0:4, :] + u0 * b0c1) + u1 * b1c1 + sk * x1
    g0 = y0 * (z0 * (1.0 / (1.0 + jnp.exp(-z0))))
    g1 = y1 * (z1 * (1.0 / (1.0 + jnp.exp(-z1))))
    width = g0.shape[1]

    def norm(g):
        ms = jnp.sum(g * g, axis=1, keepdims=True) / width
        return g * lax.rsqrt(ms + norm_eps) * norm_w[...]

    n0, n1 = norm(g0), norm(g1)
    normed = jnp.concatenate([v[k : k + 1] for k in range(4) for v in (n0, n1)], axis=0)
    nall[d] = jnp.concatenate([normed[:, :1024], normed[:, 1024:]], axis=0).astype(bf16)
    ns = []
    for o in range(1, ND):
        peer = lax.rem(d + o, ND)
        c = remote(nall.at[d], nall.at[d], n_s.at[o], n_r.at[o], "dp", peer)
        c.start()
        ns.append(c)
    sent += ns

    aa = a0 * a1
    v0 = a1 * u0
    pad256 = jnp.zeros((4, 256), f32)
    bb = jnp.concatenate([b0, b1, pad256], axis=1)
    for c in range(NT):
        q, r = c // 4, c % 4
        rows = []
        for j in range(2):
            k = 2 * q + j
            for v in (v0, u1, aa):
                rows.append(v[k : k + 1, r * 512 : (r + 1) * 512])
            rows.append(bb[k : k + 1])
        pk[c] = jnp.concatenate(rows, axis=0)
    ks = {}
    for o in range(1, NT):
        peer = lax.rem(t + o, NT)
        c = remote(pk.at[peer], pkrx.at[o], k_s.at[o], k_r.at[o], "tensor", peer)
        c.start()
        ks[o] = c
    sent += list(ks.values())

    for c in ns:
        c.wait_recv()
    blocks = []
    for s in range(ND):
        v = nall[s].astype(f32)
        blocks.append(jnp.concatenate([v[0:8], v[8:16]], axis=1))
    nmat = jnp.concatenate(blocks, axis=0).astype(bf16)
    wo_copy.wait()
    for q in range(4):
        mix = jnp.dot(nmat, wout_v[:, q * 512 : (q + 1) * 512], preferred_element_type=f32)
        emb = jnp.concatenate([full[2 * q], full[2 * q + 1]], axis=1).astype(f32)
        mixed = mix + emb
        for c in range(NT):
            mix32[c, 4 * q : 4 * q + 4, :] = mix[4 * c : 4 * c + 4]
            own32[c, 4 * q : 4 * q + 4, :] = mixed[4 * c : 4 * c + 4]
    for c in range(NT):
        mo[c] = mix32[c].astype(bf16)
    ms = []
    for o in range(1, NT):
        peer = lax.rem(t + o, NT)
        c = remote(mo.at[peer], mrx.at[o], m_s.at[o], m_r.at[o], "tensor", peer)
        c.start()
        ms.append(c)
    sent += ms

    def finish(o):
        source = lax.rem(t + NT - o, NT)
        if o == 0:
            pack = pk[t]
        else:
            p2[o].wait_recv()
            ks[o].wait_recv()
            pack = pkrx[o]
        for j in range(2):
            uh, ul = split2(pack[4 * j : 4 * j + 1])
            wh, wl = split2(pack[4 * j + 1 : 4 * j + 2])
            ah, al = split2(pack[4 * j + 2 : 4 * j + 3])
            bh, bl = split2(pack[4 * j + 3 : 4 * j + 4])
            left = jnp.concatenate(
                [uh, uh, ul, wh, wh, wl, ah, al, jnp.zeros((8, 512), f32)], axis=0
            ).astype(bf16)
            b0h, b0l, b1h, b1l = bh[:, :128], bl[:, :128], bh[:, 128:256], bl[:, 128:256]
            outer = jnp.concatenate(
                [b0h, b0l, b0h, b1h, b1l, b1h, jnp.zeros((10, 128), f32)], axis=0
            ).astype(bf16)
            row = lax.broadcasted_iota(jnp.int32, (16, 128), 0)
            ones = jnp.where((row == 6) | (row == 7), 1.0, 0.0).astype(bf16)
            right = jnp.concatenate([ones, outer], axis=1)
            g = lax.dot_general(left, right, (((0,), (0,)), ((), ())), preferred_element_type=f32)
            new = fin[o, j].astype(f32) * g[:, :128] + g[:, 128:]
            ost[o, :, j] = new.reshape(8, 64, 128)
        c = pltpu.make_async_copy(ost.at[o], ds_out.at[source], o_sem.at[o])
        c.start()
        return c

    outs = [finish(o) for o in (0, 4, 1, 5)]
    for c in ms:
        c.wait_recv()
    own = own32[t]
    for o in range(1, NT):
        own = own + mrx[o].astype(f32)
    lo_out[...] = jnp.concatenate([own[4 * q : 4 * q + 4] for q in range(4)], axis=1).astype(bf16)
    for o in (2, 6, 3, 7):
        outs.append(finish(o))
    for c in sent:
        c.wait_send()
    for c in outs:
        c.wait()


def fused(
    prefill_state, assign, tokens, embed_table, w_xz, w_dt, w_bc, dt_bias, a_log, d_skip, norm_w, w_out
):
    f32, bf16 = jnp.float32, jnp.bfloat16
    vmem = pl.BlockSpec(memory_space=pltpu.VMEM)
    smem = pl.BlockSpec(memory_space=pltpu.SMEM)
    hbm = pl.BlockSpec(memory_space=pl.ANY)
    embm, idx = pl.pallas_call(
        lookup_kernel,
        out_shape=(
            jax.ShapeDtypeStruct((8, 32, 256), bf16),
            jax.ShapeDtypeStruct((8,), jnp.int32),
        ),
        in_specs=[smem, smem, hbm],
        out_specs=(vmem, smem),
        scratch_shapes=[
            pltpu.SMEM((16,), jnp.int32),
            pltpu.VMEM((32, 16, 2048), bf16),
            pltpu.VMEM((32, 2048), f32),
            pltpu.SemaphoreType.DMA((32,)),
        ],
        compiler_params=pltpu.CompilerParams(vmem_limit_bytes=60 << 20),
    )(assign, tokens, embed_table)
    dma = pltpu.SemaphoreType.DMA
    layer_out, decode_state = pl.pallas_call(
        layer_kernel,
        out_shape=(
            jax.ShapeDtypeStruct((4, 2048), bf16),
            jax.ShapeDtypeStruct((8, 8, 2, 64, 128), f32),
        ),
        in_specs=[smem, vmem, hbm, hbm, vmem, vmem, vmem, vmem, vmem, vmem, hbm],
        out_specs=(vmem, hbm),
        scratch_shapes=[
            pltpu.VMEM((4, 4, 512, 128), f32),
            pltpu.VMEM((2048, 32, 128), bf16),
            pltpu.VMEM((2048, 2048), bf16),
            pltpu.VMEM((8, 32, 256), bf16),
            pltpu.VMEM((8, 32, 256), bf16),
            pltpu.VMEM((4, 8, 4480), f32),
            pltpu.VMEM((4, 8, 4480), f32),
            pltpu.VMEM((4, 4, 512, 128), bf16),
            pltpu.VMEM((4, 512, 128), bf16),
            pltpu.VMEM((4, 512, 128), bf16),
            pltpu.VMEM((4, 512, 128), bf16),
            pltpu.VMEM((4, 512, 128), bf16),
            pltpu.VMEM((4, 4, 512, 128), bf16),
            pltpu.VMEM((8, 2, 512, 128), bf16),
            pltpu.VMEM((2, 8, 2048), f32),
            pltpu.VMEM((4, 16, 1024), bf16),
            pltpu.VMEM((8, 16, 512), f32),
            pltpu.VMEM((8, 16, 512), f32),
            pltpu.VMEM((8, 16, 512), bf16),
            pltpu.VMEM((8, 16, 512), bf16),
            pltpu.VMEM((8, 8, 512), f32),
            pltpu.VMEM((8, 8, 512), f32),
            pltpu.VMEM((8, 8, 2, 64, 128), f32),
            dma((1,)), dma((8,)), dma((1,)),
            dma((8,)), dma((8,)), dma((8,)), dma((8,)),
            dma((4, 4)), dma((4, 4)), dma((8,)), dma((8,)),
            dma((4,)), dma((4,)), dma((4,)), dma((4,)),
            dma((8,)), dma((8,)), dma((8,)), dma((8,)), dma((8,)),
        ],
        compiler_params=pltpu.CompilerParams(
            collective_id=0, has_side_effects=True, vmem_limit_bytes=60 << 20
        ),
        cost_estimate=pl.CostEstimate(
            flops=900_000_000, bytes_accessed=40_000_000, transcendentals=100_000
        ),
    )(
        idx, embm, prefill_state.reshape(4, 4, 512, 128), w_xz, w_bc, w_dt,
        dt_bias.reshape(1, 32), a_log.reshape(1, 32), d_skip.reshape(1, 32),
        norm_w.reshape(1, 2048), w_out,
    )
    return layer_out.reshape(2, 2, 2048), decode_state.reshape(1, 1, 64, 2, 64, 128)


def solution(mesh):
    sizes = (mesh.shape["dp"], mesh.shape["tensor"])
    in_specs = (
        P("dp", "tensor", None, None),
        P(),
        P(),
        P("tensor", "dp"),
        P("dp", "tensor", None),
        P("dp", "tensor"),
        P("dp", "tensor"),
        P("tensor"),
        P("tensor"),
        P("tensor"),
        P("tensor", None),
        P("tensor", "dp"),
    )
    out_specs = (P("tensor", None, "dp"), P("dp", "tensor", None, None, None, None))
    return jax.shard_map(
        fused if sizes == (4, 8) else on_device, mesh=mesh, in_specs=in_specs, out_specs=out_specs, check_vma=False
    )
```
